512 devices in a mesh: seq: 64 (over z, y), head: 8 (over x, core).
Axes of the slice: x: 4, y: 4, z: 16, core: 2. Of those that a mesh axis runs over, the one named last changes fastest.
Arguments:
- student_query: bfloat16 [8192, 64, 576], P('seq', 'head'), may hold values from -256 to 256
- teacher_query: bfloat16 [8192, 64, 576], P('seq', 'head'), may hold values from -256 to 256
- student_keys: bfloat16 [8192, 576], P('seq'), may hold values from -4 to 4
- teacher_keys: bfloat16 [8192, 576], P('seq'), may hold values from -4 to 4
- loss_weight: float32 [8192, 64], P('seq', 'head'), may hold values from 4 to 40
- doc_lengths: int32 [16], replicated, may hold values from 1 to 896, 8192 in all
Outputs:
- query_grad: bfloat16 [8192, 64, 576], P('seq', 'head')
- key_grad: bfloat16 [8192, 576], P('seq')
The draws below stay inside these ranges and needn't reach their ends.
Inputs may be any that keep to these rules, and one draw needn't show every extreme that they name: `doc_lengths`: the lengths sum to 8192 and the longest is exactly 896.
All inputs are finite; a program needn't handle non-finite values.
Results may differ from the reference program's by a relative error of at most 0.012.
Values may be sent and summed in bfloat16 or wider, within the bound.
No kernel may reach another device: no remote copies, remote signals or barrier semaphores. Data moves between devices by JAX's collectives and lax.ppermute only.
A program may use at most 64 MiB of HBM per device.

```python
import math
import jax
import jax.numpy as jnp
import numpy as np
from jax import lax

HEADS = 64
LATENT = 512
ROPE = 64
KDIM = 576
TOK_DEV = 128
SPAN = 7
NDOC = 16
TOKENS = 8192
MAXLEN = 896


def rope_rows(key, salt):
    base = jax.random.normal(jax.random.fold_in(key, salt), (TOKENS, ROPE), jnp.float32)
    return jnp.clip(base, -4.0, 4.0)


def key_table(key, salt, fold):
    rope = rope_rows(key, salt)
    key = jax.random.fold_in(key, fold)
    latent = jnp.clip(jax.random.normal(key, (TOKENS, LATENT), jnp.float32), -4.0, 4.0)
    return (latent, rope)


def query_table(key, fold):
    key = jax.random.fold_in(key, fold)
    base = jnp.clip(jax.random.normal(key, (TOKENS, HEADS, KDIM), jnp.float32), -4.0, 4.0)
    return base


def draw_student_keys(key, part):
    latent, rope = key_table(key, 11, 1)
    return jnp.concatenate([latent, rope], axis=1).astype(jnp.bfloat16)


def draw_teacher_keys(key, part):
    latent, rope = key_table(key, 12, 3)
    return jnp.concatenate([latent, rope], axis=1).astype(jnp.bfloat16)


def draw_student_query(key, part):
    base = query_table(key, 2)
    return base.astype(jnp.bfloat16)


def draw_teacher_query(key, part):
    base = query_table(key, 4)
    return base.astype(jnp.bfloat16)


def block_levels(stream_key, shape, cuts, smallest, largest):
    level = 1.0
    for position, shards_of in cuts:
        heights = jax.random.uniform(jax.random.fold_in(jax.random.fold_in(stream_key, 6), position), (shards_of,), jnp.float32, smallest / len(cuts), largest / len(cuts))
        level = level * jnp.repeat(jnp.exp(heights), shape[position] // shards_of).reshape((-1,) + (1,) * (len(shape) - 1 - position))
    return level


def length_profile(number_of, total, most, slope):
    loads = [(1 << 20) // math.isqrt(grade ** slope) + 1 for grade in range(2, number_of + 1)]
    rest, counts = total - most - (number_of - 1), [1] * (number_of - 1)
    while rest > 0:
        free = [i for i in range(number_of - 1) if counts[i] < most]
        whole, remaining = sum([loads[i] for i in free]), rest
        for i in free:
            addition = min(most - counts[i], max(1, remaining * loads[i] // whole), rest)
            counts[i] = counts[i] + addition
            rest = rest - addition
    return np.array([most] + counts)


def uneven(stream_key, count, total, reach, lean):
    if count == 2:
        one = jax.random.randint(stream_key, (), max(1, total - reach), min(reach, total - 1) + 1)
        return jnp.stack([one, total - one])
    lengths = jnp.asarray(length_profile(count, total, reach, lean), jnp.int32)
    couples = (count - 1) // 2
    donor, receiver = lengths[1:1 + 2 * couples:2], lengths[2:2 + 2 * couples:2]
    room = jnp.minimum(donor - 1, reach - receiver)
    shifted = jax.random.randint(jax.random.fold_in(stream_key, 1), (couples,), 0, 1 << 20) % (room + 1)
    lengths = lengths.at[1:1 + 2 * couples:2].set(donor - shifted).at[2:2 + 2 * couples:2].set(receiver + shifted)
    return lengths[jax.random.permutation(jax.random.fold_in(stream_key, 2), count)]


def setup_inputs(seed: int = 0) -> dict:
    key_of = jax.random.split(jax.random.key(seed), 7)
    return {
        "student_query": draw_student_query(jax.random.fold_in(key_of[6], 71), 0),
        "teacher_query": draw_teacher_query(jax.random.fold_in(key_of[6], 71), 0),
        "student_keys": draw_student_keys(jax.random.fold_in(key_of[6], 71), 0),
        "teacher_keys": draw_teacher_keys(jax.random.fold_in(key_of[6], 71), 0),
        "loss_weight": jnp.clip(jnp.exp(math.log(40.0) - 2.3025851 * jax.random.uniform(key_of[4], (TOKENS, HEADS), jnp.float32) ** block_levels(key_of[4], (TOKENS, HEADS), ((0, 64), (1, 8)), -0.2, 0.2)), 4.0, 40.0),
        "doc_lengths": uneven(key_of[5], NDOC, TOKENS, MAXLEN, 2).astype(jnp.int32),
    }


score_scale = 192.0 ** -0.5


def doc_index(positions, doc_lengths):
    ends = jnp.cumsum(doc_lengths.astype(jnp.int32)).astype(jnp.int32)
    return jnp.sum((positions[:, None] >= ends[None, :]).astype(jnp.int32), axis=1)


def masked_softmax(scores, visible):
    peak = jnp.max(jnp.where(visible, scores, -jnp.inf), axis=-1, keepdims=True)
    expo = jnp.where(visible, jnp.exp(scores - peak), 0.0)
    return expo / jnp.sum(expo, axis=-1, keepdims=True)


def reference(student_query, teacher_query, student_keys, teacher_keys, loss_weight, doc_lengths):
    window = (SPAN + 1) * TOK_DEV
    front = SPAN * TOK_DEV
    pad_keys = jnp.zeros((front, KDIM), jnp.bfloat16)
    student_pad = jnp.concatenate([pad_keys, student_keys], axis=0)
    teacher_pad = jnp.concatenate([pad_keys, teacher_keys], axis=0)
    blocks = TOKENS // TOK_DEV

    def one_block(carry, block):
        start = (block * TOK_DEV).astype(jnp.int32)
        query_s = lax.dynamic_slice_in_dim(student_query, start, TOK_DEV, 0).astype(jnp.float32)
        query_t = lax.dynamic_slice_in_dim(teacher_query, start, TOK_DEV, 0).astype(jnp.float32)
        weights = lax.dynamic_slice_in_dim(loss_weight, start, TOK_DEV, 0)
        keys_s = lax.dynamic_slice_in_dim(student_pad, start, window, 0).astype(jnp.float32)
        keys_t = lax.dynamic_slice_in_dim(teacher_pad, start, window, 0).astype(jnp.float32)
        query_pos = start + jnp.arange(TOK_DEV, dtype=jnp.int32)
        key_pos = start - front + jnp.arange(window, dtype=jnp.int32)
        query_doc = doc_index(query_pos, doc_lengths)
        key_doc = doc_index(key_pos, doc_lengths)
        visible = (query_doc[:, None] == key_doc[None, :]) & (key_pos[None, :] <= query_pos[:, None]) & (key_pos[None, :] >= 0)
        visible = visible[:, None, :]
        student_scores = jnp.einsum('thc,kc->thk', query_s, keys_s) * score_scale
        teacher_scores = jnp.einsum('thc,kc->thk', query_t, keys_t) * score_scale
        student_probs = masked_softmax(student_scores, visible)
        teacher_probs = masked_softmax(teacher_scores, visible)
        score_grad = (weights[:, :, None] * (student_probs - teacher_probs) * score_scale).astype(jnp.bfloat16)
        grad_f = score_grad.astype(jnp.float32)
        query_grad = jnp.einsum('thk,kc->thc', grad_f, keys_s).astype(jnp.bfloat16)
        key_terms = jnp.einsum('thk,thc->kc', grad_f, query_s)
        current = lax.dynamic_slice_in_dim(carry, start, window, 0)
        carry = lax.dynamic_update_slice_in_dim(carry, current + key_terms, start, 0)
        return carry, query_grad

    init = jnp.zeros((front + TOKENS, KDIM), jnp.float32)
    summed, query_blocks = lax.scan(one_block, init, jnp.arange(blocks, dtype=jnp.int32))
    query_grad = query_blocks.reshape(TOKENS, HEADS, KDIM)
    key_grad = summed[front:].astype(jnp.bfloat16)
    return query_grad, key_grad
```

```python
import math

import jax
import jax.numpy as jnp
from jax import lax
from jax.experimental import pallas as pl
from jax.experimental.pallas import tpu as pltpu
from jax.sharding import Mesh
from jax.sharding import PartitionSpec as P

SEQ_GROUP = 8
TOK = 128
WIN = SEQ_GROUP * TOK
KDIM = 576
HALF = KDIM // 2
PIECE = KDIM // 4
HEADS = 8
SCALE = 192.0 ** (-0.5)
SCALE_LOG2 = SCALE * math.log2(math.e)
HIDDEN = -1e30
VMEM = 48 * 1024 * 1024


def key_rows(kt_ref, k_ref):
    for j in range(SEQ_GROUP):
        k_ref[j * TOK : (j + 1) * TOK, :] = kt_ref[j].T


def hidden_bias(meta, bias_ref):
    me, seq = meta[1], meta[2]
    query_pos = seq * TOK + lax.broadcasted_iota(jnp.int32, (1, TOK), 1)
    start = jnp.zeros((1, TOK), jnp.int32)
    end = jnp.int32(0)
    for m in range(16):
        end = end + meta[3 + m]
        start = jnp.where(query_pos >= end, end, start)
    row = lax.broadcasted_iota(jnp.int32, (TOK, TOK), 0)
    for j in range(SEQ_GROUP):
        block = seq - me + j - jnp.where(j > me, SEQ_GROUP, 0)
        key_pos = block * TOK + row
        seen = (key_pos >= start) & (key_pos <= query_pos)
        bias_ref[j * TOK : (j + 1) * TOK, :] = jnp.where(seen, 0.0, HIDDEN)


def both(a, b):
    return jnp.concatenate([a, b], axis=1)


def exponentials(k_ref, bias_ref, queries, s_ref):
    s_ref[...] = jnp.dot(k_ref[...], queries, preferred_element_type=jnp.float32)
    peak = jnp.full((8, 2 * TOK), HIDDEN, jnp.float32)
    for j in range(SEQ_GROUP):
        rows = slice(j * TOK, (j + 1) * TOK)
        bias = bias_ref[rows, :]
        s = s_ref[rows, :] + both(bias, bias)
        s_ref[rows, :] = s
        peak = jnp.maximum(peak, jnp.max(s.reshape(TOK // 8, 8, 2 * TOK), axis=0))
    peak = jnp.max(peak, axis=0, keepdims=True)
    total = jnp.zeros((8, 2 * TOK), jnp.float32)
    for j in range(SEQ_GROUP):
        rows = slice(j * TOK, (j + 1) * TOK)
        e = jnp.exp2((s_ref[rows, :] - peak) * SCALE_LOG2)
        s_ref[rows, :] = e
        total = total + jnp.sum(e.reshape(TOK // 8, 8, 2 * TOK), axis=0)
    return jnp.sum(total, axis=0, keepdims=True)


def pair_weight(lw_ref, i):
    return both(lw_ref[pl.ds(2 * i, 1), :], lw_ref[pl.ds(2 * i + 1, 1), :]) * SCALE


def first_kernel(meta, kt_ref, sq_ref, tq_ref, lw_ref, p_ref, k_ref, bias_ref, s_ref):
    i = pl.program_id(0)
    core = meta[0]

    @pl.when(i == 0)
    def _():
        key_rows(kt_ref, k_ref)
        hidden_bias(meta, bias_ref)

    student = core == 0
    queries = both(
        jnp.where(student, sq_ref[0], tq_ref[0]), jnp.where(student, sq_ref[1], tq_ref[1])
    )
    total = exponentials(k_ref, bias_ref, queries, s_ref)
    factor = pair_weight(lw_ref, i) / total
    for j in range(SEQ_GROUP):
        rows = slice(j * TOK, (j + 1) * TOK)
        p_ref[rows, :] = s_ref[rows, :] * factor


def second_kernel(
    meta, kt_ref, sq_ref, tq_ref, lw_ref, p_ref, sh_ref, g_ref, kg_ref, k_ref, bias_ref, s_ref, all_ref
):
    i = pl.program_id(0)
    core = meta[0]

    @pl.when(i == 0)
    def _():
        key_rows(kt_ref, k_ref)
        hidden_bias(meta, bias_ref)

    student = core == 1
    queries = both(
        jnp.where(student, sq_ref[0], tq_ref[0]), jnp.where(student, sq_ref[1], tq_ref[1])
    )
    total = exponentials(k_ref, bias_ref, queries, s_ref)
    factor = pair_weight(lw_ref, i) / total
    sign = jnp.where(student, -1.0, 1.0)
    lanes = pl.ds(pl.multiple_of(i * 2 * TOK, 2 * TOK), 2 * TOK)
    for j in range(SEQ_GROUP):
        rows = slice(j * TOK, (j + 1) * TOK)
        g = ((p_ref[rows, :] - s_ref[rows, :] * factor) * sign).astype(jnp.bfloat16)
        g_ref[rows, :] = g
        all_ref[rows, lanes] = g

    @pl.when(i == HEADS // 2 - 1)
    def _():
        half = jnp.concatenate([sh_ref[h] for h in range(HEADS)], axis=1)
        for j in range(SEQ_GROUP // 2):
            grad = lax.dot_general(
                half,
                all_ref[j * 2 * TOK : (j + 1) * 2 * TOK, :],
                (((1,), (1,)), ((), ())),
                preferred_element_type=jnp.float32,
            ).astype(jnp.bfloat16)
            kg_ref[2 * j] = grad[:, :TOK]
            kg_ref[2 * j + 1] = grad[:, TOK:]


def query_kernel(meta, mine_ref, other_ref, g_ref, out_ref, kt_ref):
    @pl.when(pl.program_id(0) == 0)
    def _():
        @pl.when(meta[0] == 0)
        def _():
            for j in range(SEQ_GROUP):
                kt_ref[:, j * TOK : (j + 1) * TOK] = mine_ref[j]

        @pl.when(meta[0] == 1)
        def _():
            for j in range(SEQ_GROUP):
                kt_ref[:, j * TOK : (j + 1) * TOK] = other_ref[j]

    grad = jnp.dot(kt_ref[...], g_ref[...], preferred_element_type=jnp.float32).astype(jnp.bfloat16)
    out_ref[0] = grad[:, :TOK]
    out_ref[1] = grad[:, TOK:]


def key_kernel(meta, sh_ref, g_ref, got_ref, out_ref):
    half = jnp.concatenate([sh_ref[h] for h in range(HEADS)], axis=1)
    grad = lax.dot_general(
        half, g_ref[...], (((1,), (1,)), ((), ())), preferred_element_type=jnp.float32
    )
    out_ref[0] = (grad[:, :TOK] + got_ref[0].astype(jnp.float32)).astype(jnp.bfloat16)
    out_ref[1] = (grad[:, TOK:] + got_ref[1].astype(jnp.float32)).astype(jnp.bfloat16)


def call(kernel, grid, in_specs, out_specs, out_shape, scratch, flops, args):
    return pl.pallas_call(
        kernel,
        grid_spec=pltpu.PrefetchScalarGridSpec(
            num_scalar_prefetch=1,
            grid=(grid,),
            in_specs=in_specs,
            out_specs=out_specs,
            scratch_shapes=scratch,
        ),
        out_shape=out_shape,
        compiler_params=pltpu.CompilerParams(vmem_limit_bytes=VMEM),
        cost_estimate=pl.CostEstimate(flops=flops, bytes_accessed=8 << 20, transcendentals=1 << 20),
    )(*args)


def on_device(student_query, teacher_query, student_keys, teacher_keys, loss_weight, doc_lengths):
    core = lax.axis_index("c")
    x = lax.axis_index("x")
    me = lax.axis_index(("zi", "y"))
    seq = lax.axis_index(("zo", "zi", "y"))
    meta = jnp.concatenate([jnp.stack([core, me, seq]).astype(jnp.int32), doc_lengths])
    sq = student_query.transpose(1, 2, 0)
    tq = teacher_query.transpose(1, 2, 0)
    lw = loss_weight.T

    table = jnp.where(core == 0, student_keys.T, teacher_keys.T)
    own = lax.dynamic_slice_in_dim(table, x * PIECE, PIECE, 0)
    before = lax.ppermute(own, ("zo", "zi"), [(i, (i + 2) % 16) for i in range(16)])
    later = (jnp.arange(SEQ_GROUP) >= me)[:, None, None, None]
    outgoing = jnp.broadcast_to(jnp.where(later, own, before), (SEQ_GROUP, 4, PIECE, TOK))
    mine = lax.all_to_all(
        outgoing.reshape(SEQ_GROUP * 4, PIECE, TOK), ("zi", "y", "x"), 0, 0, tiled=True
    ).reshape(SEQ_GROUP, KDIM, TOK)
    other = lax.ppermute(mine, "c", [(0, 1), (1, 0)])

    whole_keys = pl.BlockSpec((SEQ_GROUP, KDIM, TOK), lambda i, m: (0, 0, 0))
    on_first = pl.BlockSpec((2, KDIM, TOK), lambda i, m: (i * (1 - m[0]), 0, 0))
    on_second = pl.BlockSpec((2, KDIM, TOK), lambda i, m: (i * m[0], 0, 0))
    weights = pl.BlockSpec((HEADS, TOK), lambda i, m: (0, 0))
    pair = pl.BlockSpec((WIN, 2 * TOK), lambda i, m: (0, i))
    scratch = [
        pltpu.VMEM((WIN, KDIM), jnp.bfloat16),
        pltpu.VMEM((WIN, TOK), jnp.float32),
        pltpu.VMEM((WIN, 2 * TOK), jnp.float32),
    ]
    matmul = 2 * WIN * HEADS * TOK * KDIM
    probs = call(
        first_kernel,
        HEADS // 2,
        [whole_keys, on_first, on_second, weights],
        pair,
        jax.ShapeDtypeStruct((WIN, HEADS * TOK), jnp.float32),
        scratch,
        matmul,
        (meta, mine, sq, tq, lw),
    )
    score_grad, sent = call(
        second_kernel,
        HEADS // 2,
        [
            whole_keys,
            on_second,
            on_first,
            weights,
            pair,
            pl.BlockSpec((HEADS, HALF, TOK), lambda i, m: (0, 1 - m[0], 0)),
        ],
        [pair, pl.BlockSpec((SEQ_GROUP, HALF, TOK), lambda i, m: (0, 0, 0))],
        [
            jax.ShapeDtypeStruct((WIN, HEADS * TOK), jnp.bfloat16),
            jax.ShapeDtypeStruct((SEQ_GROUP, HALF, TOK), jnp.bfloat16),
        ],
        scratch + [pltpu.VMEM((WIN, HEADS * TOK), jnp.bfloat16)],
        matmul * 3 // 2,
        (meta, other, sq, tq, lw, probs, sq),
    )
    got = lax.ppermute(sent, "c", [(0, 1), (1, 0)])
    query_grad = call(
        query_kernel,
        HEADS // 2,
        [whole_keys, whole_keys, pair],
        pl.BlockSpec((2, KDIM, TOK), lambda i, m: (i, 0, 0)),
        jax.ShapeDtypeStruct((HEADS, KDIM, TOK), jnp.bfloat16),
        [pltpu.VMEM((KDIM, WIN), jnp.bfloat16)],
        matmul,
        (meta, mine, other, score_grad),
    )
    two_blocks = pl.BlockSpec((2, HALF, TOK), lambda i, m: (i, 0, 0))
    partial = call(
        key_kernel,
        SEQ_GROUP // 2,
        [
            pl.BlockSpec((HEADS, HALF, TOK), lambda i, m: (0, m[0], 0)),
            pl.BlockSpec((2 * TOK, HEADS * TOK), lambda i, m: (i, 0)),
            two_blocks,
        ],
        two_blocks,
        jax.ShapeDtypeStruct((SEQ_GROUP, HALF, TOK), jnp.bfloat16),
        [],
        matmul // 2,
        (meta, sq, score_grad, got),
    )
    rows = HALF // 4
    terms = lax.all_to_all(
        partial.reshape(SEQ_GROUP * 4, rows, TOK), ("zi", "y", "x"), 0, 0, tiled=True
    ).reshape(SEQ_GROUP, 4, rows, TOK)
    terms = jnp.sum(terms.astype(jnp.float32), axis=1)
    here = (jnp.arange(SEQ_GROUP) >= me)[:, None, None]
    kept = jnp.sum(jnp.where(here, terms, 0.0), axis=0)
    returned = jnp.sum(jnp.where(here, 0.0, terms), axis=0)
    returned = lax.ppermute(returned, ("zo", "zi"), [(i, (i - 2) % 16) for i in range(16)])
    share = (kept + returned).astype(jnp.bfloat16)
    key_grad = lax.all_to_all(
        jnp.broadcast_to(share, (8, rows, TOK)), ("c", "x"), 0, 0, tiled=True
    ).reshape(KDIM, TOK)
    return (query_grad.transpose(2, 0, 1), key_grad.T)


def solution(mesh):
    fine = Mesh(mesh.devices.reshape(8, 2, 4, 4, 2), ("zo", "zi", "y", "x", "c"))
    seq, head = ("zo", "zi", "y"), ("x", "c")
    return jax.shard_map(
        on_device,
        mesh=fine,
        in_specs=(
            P(seq, head, None),
            P(seq, head, None),
            P(seq, None),
            P(seq, None),
            P(seq, head),
            P(),
        ),
        out_specs=(P(seq, head, None), P(seq, None)),
        check_vma=False,
    )
```

```python
import math

import jax
import jax.numpy as jnp
from jax import lax
from jax.experimental import pallas as pl
from jax.experimental.pallas import tpu as pltpu
from jax.sharding import Mesh
from jax.sharding import PartitionSpec as P

SEQ_GROUP = 8
TOK = 128
WIN = SEQ_GROUP * TOK
KDIM = 576
HALF = KDIM // 2
PIECE = KDIM // 4
HEADS = 8
PAIRS = HEADS // 2
BLOCKS = [slice(j * TOK, (j + 1) * TOK) for j in range(SEQ_GROUP)]
SCALE = 192.0 ** (-0.5)
SCALE_LOG2 = SCALE * math.log2(math.e)
HIDDEN = -1e30


def key_rows(kt_ref, k_ref):
    for j in range(SEQ_GROUP):
        k_ref[j * TOK : (j + 1) * TOK, :] = kt_ref[j].T


def hidden_bias(meta, bias_ref):
    me, seq = meta[1], meta[2]
    query_pos = seq * TOK + lax.broadcasted_iota(jnp.int32, (1, TOK), 1)
    start = jnp.zeros((1, TOK), jnp.int32)
    end = jnp.int32(0)
    for m in range(16):
        end = end + meta[3 + m]
        start = jnp.where(query_pos >= end, end, start)
    row = lax.broadcasted_iota(jnp.int32, (TOK, TOK), 0)
    for j in range(SEQ_GROUP):
        block = seq - me + j - jnp.where(j > me, SEQ_GROUP, 0)
        key_pos = block * TOK + row
        seen = (key_pos >= start) & (key_pos <= query_pos)
        bias_ref[j * TOK : (j + 1) * TOK, :] = jnp.where(seen, 0.0, HIDDEN)


def both(a, b):
    return jnp.concatenate([a, b], axis=1)


def scores(k_ref, bias_ref, queries, s_ref):
    s_ref[...] = jnp.dot(k_ref[...], queries, preferred_element_type=jnp.float32)
    peak = jnp.full((8, 2 * TOK), HIDDEN, jnp.float32)
    for rows in BLOCKS:
        bias = bias_ref[rows, :]
        s = s_ref[rows, :] + both(bias, bias)
        s_ref[rows, :] = s
        peak = jnp.maximum(peak, jnp.max(s.reshape(TOK // 8, 8, 2 * TOK), axis=0))
    return jnp.max(peak, axis=0, keepdims=True)


def exponentials(s_ref, peak):
    total = jnp.zeros((8, 2 * TOK), jnp.float32)
    for rows in BLOCKS:
        e = jnp.exp2((s_ref[rows, :] - peak) * SCALE_LOG2)
        s_ref[rows, :] = e
        total = total + jnp.sum(e.reshape(TOK // 8, 8, 2 * TOK), axis=0)
    return jnp.sum(total, axis=0, keepdims=True)


def pair_queries(student, sq_ref, tq_ref, i):
    return both(
        jnp.where(student, sq_ref[2 * i], tq_ref[2 * i]),
        jnp.where(student, sq_ref[2 * i + 1], tq_ref[2 * i + 1]),
    )


def pair_weight(lw_ref, i, student):
    weight = both(lw_ref[2 * i : 2 * i + 1, :], lw_ref[2 * i + 1 : 2 * i + 2, :])
    return weight * jnp.where(student, SCALE, -SCALE)


def all_pairs(meta, student, kt_ref, sq_ref, tq_ref, lw_ref, k_ref, bias_ref, s_ref, use):
    key_rows(kt_ref, k_ref)
    hidden_bias(meta, bias_ref)
    peak = scores(k_ref, bias_ref, pair_queries(student, sq_ref, tq_ref, 0), s_ref.at[0])
    for i in range(PAIRS):
        later = None
        if i + 1 < PAIRS:
            queries = pair_queries(student, sq_ref, tq_ref, i + 1)
            later = scores(k_ref, bias_ref, queries, s_ref.at[(i + 1) % 2])
        total = exponentials(s_ref.at[i % 2], peak)
        factor = pair_weight(lw_ref, i, student) / total
        for rows in BLOCKS:
            use(i, rows, s_ref[i % 2, rows, :] * factor)
        peak = later


def pair_lanes(i):
    return slice(i * 2 * TOK, (i + 1) * 2 * TOK)


def first_kernel(meta, kt_ref, sq_ref, tq_ref, lw_ref, p_ref, k_ref, bias_ref, s_ref):
    def use(i, rows, probs):
        p_ref[rows, pair_lanes(i)] = probs

    student = meta[0] == 0
    all_pairs(meta, student, kt_ref, sq_ref, tq_ref, lw_ref, k_ref, bias_ref, s_ref, use)


def key_grad_half(sq_ref, half, g):
    rows = pl.ds(pl.multiple_of(half * HALF, HALF), HALF)
    queries = jnp.concatenate([sq_ref[h, rows, :] for h in range(HEADS)], axis=1)
    return lax.dot_general(
        queries, g, (((1,), (1,)), ((), ())), preferred_element_type=jnp.float32
    )


def second_kernel(
    meta, kt_ref, sq_ref, tq_ref, lw_ref, p_ref, g_ref, kg_ref, k_ref, bias_ref, s_ref
):
    student = meta[0] == 1

    def use(i, rows, probs):
        g_ref[rows, pair_lanes(i)] = (p_ref[rows, pair_lanes(i)] + probs).astype(jnp.bfloat16)

    all_pairs(meta, student, kt_ref, sq_ref, tq_ref, lw_ref, k_ref, bias_ref, s_ref, use)
    grad = key_grad_half(sq_ref, 1 - meta[0], g_ref[...]).astype(jnp.bfloat16)
    for j in range(SEQ_GROUP):
        kg_ref[j] = grad[:, j * TOK : (j + 1) * TOK]


def query_kernel(
    meta, mine_ref, other_ref, g_ref, kept_ref, out_ref, kept_out_ref, kt_ref, stage_ref, sems
):
    kept_out_ref[...] = kept_ref[...]

    @pl.when(meta[0] == 0)
    def _():
        for j in range(SEQ_GROUP):
            kt_ref[:, j * TOK : (j + 1) * TOK] = mine_ref[j]

    @pl.when(meta[0] == 1)
    def _():
        for j in range(SEQ_GROUP):
            kt_ref[:, j * TOK : (j + 1) * TOK] = other_ref[j]

    copies = []
    for i in range(PAIRS):
        grad = jnp.dot(
            kt_ref[...], g_ref[:, pair_lanes(i)], preferred_element_type=jnp.float32
        ).astype(jnp.bfloat16)
        stage_ref[2 * i] = grad[:, :TOK]
        stage_ref[2 * i + 1] = grad[:, TOK:]
        pair = pl.ds(2 * i, 2)
        copies.append(pltpu.make_async_copy(stage_ref.at[pair], out_ref.at[pair], sems.at[i]))
        copies[-1].start()
    for copy in copies:
        copy.wait()


def key_kernel(meta, sq_ref, g_ref, got_ref, out_ref):
    grad = key_grad_half(sq_ref, meta[0], g_ref[...])
    for j in range(SEQ_GROUP):
        lanes = slice(j * TOK, (j + 1) * TOK)
        out_ref[j] = (grad[:, lanes] + got_ref[j].astype(jnp.float32)).astype(jnp.bfloat16)


def call(kernel, out_specs, out_shape, scratch, mib, flops, args):
    in_vmem = pl.BlockSpec(memory_space=pltpu.VMEM)
    return pl.pallas_call(
        kernel,
        in_specs=[pl.BlockSpec(memory_space=pltpu.SMEM)] + [in_vmem] * (len(args) - 1),
        out_specs=out_specs,
        out_shape=out_shape,
        scratch_shapes=scratch,
        compiler_params=pltpu.CompilerParams(vmem_limit_bytes=mib << 20),
        cost_estimate=pl.CostEstimate(flops=flops, bytes_accessed=8 << 20, transcendentals=1 << 20),
    )(*args)


def on_device(student_query, teacher_query, student_keys, teacher_keys, loss_weight, doc_lengths):
    core = lax.axis_index("c")
    x = lax.axis_index("x")
    me = lax.axis_index(("zi", "y"))
    seq = lax.axis_index(("zo", "zi", "y"))
    meta = jnp.concatenate([jnp.stack([core, me, seq]).astype(jnp.int32), doc_lengths])
    sq = student_query.transpose(1, 2, 0)
    tq = teacher_query.transpose(1, 2, 0)
    lw = loss_weight.T

    table = jnp.where(core == 0, student_keys.T, teacher_keys.T)
    own = lax.dynamic_slice_in_dim(table, x * PIECE, PIECE, 0)
    before = lax.ppermute(own, ("zo", "zi"), [(i, i + 2) for i in range(14)])
    later = (jnp.arange(SEQ_GROUP) >= me)[:, None, None, None]
    outgoing = jnp.broadcast_to(jnp.where(later, own, before), (SEQ_GROUP, 4, PIECE, TOK))
    mine = lax.all_to_all(
        outgoing.reshape(SEQ_GROUP * 4, PIECE, TOK), ("zi", "y", "x"), 0, 0, tiled=True
    ).reshape(SEQ_GROUP, KDIM, TOK)
    other = lax.ppermute(mine, "c", [(0, 1), (1, 0)])

    in_vmem = pl.BlockSpec(memory_space=pltpu.VMEM)
    scratch = [
        pltpu.VMEM((WIN, KDIM), jnp.bfloat16),
        pltpu.VMEM((WIN, TOK), jnp.float32),
        pltpu.VMEM((2, WIN, 2 * TOK), jnp.float32),
    ]
    matmul = 2 * WIN * HEADS * TOK * KDIM
    probs = call(
        first_kernel,
        in_vmem,
        jax.ShapeDtypeStruct((WIN, HEADS * TOK), jnp.float32),
        scratch,
        12,
        matmul,
        (meta, mine, sq, tq, lw),
    )
    half_grad = jax.ShapeDtypeStruct((SEQ_GROUP, HALF, TOK), jnp.bfloat16)
    score_grad, sent = call(
        second_kernel,
        [in_vmem, in_vmem],
        [jax.ShapeDtypeStruct((WIN, HEADS * TOK), jnp.bfloat16), half_grad],
        scratch,
        12,
        matmul * 3 // 2,
        (meta, other, sq, tq, lw, probs),
    )
    got = lax.ppermute(sent, "c", [(0, 1), (1, 0)])
    partial = call(key_kernel, in_vmem, half_grad, [], 6, matmul // 2, (meta, sq, score_grad, got))
    rows = HALF // 4
    terms = lax.all_to_all(
        partial.reshape(SEQ_GROUP * 4, rows, TOK), ("zi", "y", "x"), 0, 0, tiled=True
    ).reshape(SEQ_GROUP, 4, rows, TOK)
    terms = jnp.sum(terms.astype(jnp.float32), axis=1)
    here = (jnp.arange(SEQ_GROUP) >= me)[:, None, None]
    kept = jnp.sum(jnp.where(here, terms, 0.0), axis=0)
    returned = jnp.sum(jnp.where(here, 0.0, terms), axis=0)
    returned = lax.ppermute(returned, ("zo", "zi"), [(i + 2, i) for i in range(14)])
    query_grad, kept = call(
        query_kernel,
        [pl.BlockSpec(memory_space=pl.ANY), in_vmem],
        [
            jax.ShapeDtypeStruct((HEADS, KDIM, TOK), jnp.bfloat16),
            jax.ShapeDtypeStruct((rows, TOK), jnp.float32),
        ],
        [
            pltpu.VMEM((KDIM, WIN), jnp.bfloat16),
            pltpu.VMEM((HEADS, KDIM, TOK), jnp.bfloat16),
            pltpu.SemaphoreType.DMA((PAIRS,)),
        ],
        8,
        matmul,
        (meta, mine, other, score_grad, kept),
    )
    share = (kept + returned).astype(jnp.bfloat16)
    key_grad = lax.all_to_all(
        jnp.broadcast_to(share, (8, rows, TOK)), ("c", "x"), 0, 0, tiled=True
    ).reshape(KDIM, TOK)
    return (query_grad.transpose(2, 0, 1), key_grad.T)


def solution(mesh):
    fine = Mesh(mesh.devices.reshape(8, 2, 4, 4, 2), ("zo", "zi", "y", "x", "c"))
    seq, head = ("zo", "zi", "y"), ("x", "c")
    return jax.shard_map(
        on_device,
        mesh=fine,
        in_specs=(
            P(seq, head, None),
            P(seq, head, None),
            P(seq, None),
            P(seq, None),
            P(seq, head),
            P(),
        ),
        out_specs=(P(seq, head, None), P(seq, None)),
        check_vma=False,
    )
```

```python
import math

import jax
import jax.numpy as jnp
from jax import lax
from jax.experimental import pallas as pl
from jax.experimental.pallas import tpu as pltpu
from jax.sharding import Mesh
from jax.sharding import PartitionSpec as P

SEQ_GROUP = 8
TOK = 128
WIN = SEQ_GROUP * TOK
KDIM = 576
HALF = KDIM // 2
PIECE = KDIM // 4
HEADS = 8
PAIRS = HEADS // 2
BLOCKS = [slice(j * TOK, (j + 1) * TOK) for j in range(SEQ_GROUP)]
SCALE = 192.0 ** (-0.5)
SCALE_LOG2 = SCALE * math.log2(math.e)
HIDDEN = -1e30


def key_rows(kt_ref, k_ref):
    for j in range(SEQ_GROUP):
        k_ref[j * TOK : (j + 1) * TOK, :] = kt_ref[j].T


def hidden_bias(meta, bias_ref):
    me, seq = meta[1], meta[2]
    query_pos = seq * TOK + lax.broadcasted_iota(jnp.int32, (1, TOK), 1)
    start = jnp.zeros((1, TOK), jnp.int32)
    end = jnp.int32(0)
    for m in range(16):
        end = end + meta[3 + m]
        start = jnp.where(query_pos >= end, end, start)
    row = lax.broadcasted_iota(jnp.int32, (TOK, TOK), 0)
    for j in range(SEQ_GROUP):
        block = seq - me + j - jnp.where(j > me, SEQ_GROUP, 0)
        key_pos = block * TOK + row
        seen = (key_pos >= start) & (key_pos <= query_pos)
        bias_ref[j * TOK : (j + 1) * TOK, :] = jnp.where(seen, 0.0, HIDDEN)


def both(a, b):
    return jnp.concatenate([a, b], axis=1)


def scores(k_ref, bias_ref, queries, s_ref):
    peak = jnp.full((8, 2 * TOK), HIDDEN, jnp.float32)
    for rows in BLOCKS:
        bias = bias_ref[rows, :]
        s = jnp.dot(k_ref[rows, :], queries, preferred_element_type=jnp.float32)
        s = s + both(bias, bias)
        s_ref[rows, :] = s
        peak = jnp.maximum(peak, jnp.max(s.reshape(TOK // 8, 8, 2 * TOK), axis=0))
    return jnp.max(peak, axis=0, keepdims=True)


def exponentials(s_ref, peak):
    total = jnp.zeros((8, 2 * TOK), jnp.float32)
    for rows in BLOCKS:
        e = jnp.exp2((s_ref[rows, :] - peak) * SCALE_LOG2)
        s_ref[rows, :] = e
        total = total + jnp.sum(e.reshape(TOK // 8, 8, 2 * TOK), axis=0)
    return jnp.sum(total, axis=0, keepdims=True)


def pair_queries(student, sq_ref, tq_ref, i):
    return both(
        jnp.where(student, sq_ref[2 * i], tq_ref[2 * i]),
        jnp.where(student, sq_ref[2 * i + 1], tq_ref[2 * i + 1]),
    )


def pair_weight(lw_ref, i, student):
    weight = both(lw_ref[2 * i : 2 * i + 1, :], lw_ref[2 * i + 1 : 2 * i + 2, :])
    return weight * jnp.where(student, SCALE, -SCALE)


def all_pairs(meta, student, kt_ref, sq_ref, tq_ref, lw_ref, k_ref, bias_ref, s_ref, use):
    key_rows(kt_ref, k_ref)
    hidden_bias(meta, bias_ref)
    peak = scores(k_ref, bias_ref, pair_queries(student, sq_ref, tq_ref, 0), s_ref.at[0])
    for i in range(PAIRS):
        later = None
        if i + 1 < PAIRS:
            queries = pair_queries(student, sq_ref, tq_ref, i + 1)
            later = scores(k_ref, bias_ref, queries, s_ref.at[(i + 1) % 2])
        total = exponentials(s_ref.at[i % 2], peak)
        factor = pair_weight(lw_ref, i, student) / total
        for rows in BLOCKS:
            use(i, rows, s_ref[i % 2, rows, :] * factor)
        peak = later


def pair_lanes(i):
    return slice(i * 2 * TOK, (i + 1) * 2 * TOK)


def first_kernel(meta, kt_ref, sq_ref, tq_ref, lw_ref, p_ref, k_ref, bias_ref, s_ref):
    def use(i, rows, probs):
        p_ref[rows, pair_lanes(i)] = probs

    student = meta[0] == 0
    all_pairs(meta, student, kt_ref, sq_ref, tq_ref, lw_ref, k_ref, bias_ref, s_ref, use)


def key_grad_half(sq_ref, half, g):
    rows = pl.ds(pl.multiple_of(half * HALF, HALF), HALF)
    queries = jnp.concatenate([sq_ref[h, rows, :] for h in range(HEADS)], axis=1)
    return lax.dot_general(
        queries, g, (((1,), (1,)), ((), ())), preferred_element_type=jnp.float32
    )


def second_kernel(
    meta, kt_ref, sq_ref, tq_ref, lw_ref, p_ref, g_ref, kg_ref, k_ref, bias_ref, s_ref
):
    student = meta[0] == 1

    def use(i, rows, probs):
        g_ref[rows, pair_lanes(i)] = (p_ref[rows, pair_lanes(i)] + probs).astype(jnp.bfloat16)

    all_pairs(meta, student, kt_ref, sq_ref, tq_ref, lw_ref, k_ref, bias_ref, s_ref, use)
    grad = key_grad_half(sq_ref, 1 - meta[0], g_ref[...]).astype(jnp.bfloat16)
    for j in range(SEQ_GROUP):
        kg_ref[j] = grad[:, j * TOK : (j + 1) * TOK]


def query_kernel(
    meta, mine_ref, other_ref, g_ref, kept_ref, out_ref, kept_out_ref, kt_ref, stage_ref, sems
):
    kept_out_ref[...] = kept_ref[...]

    @pl.when(meta[0] == 0)
    def _():
        for j in range(SEQ_GROUP):
            kt_ref[:, j * TOK : (j + 1) * TOK] = mine_ref[j]

    @pl.when(meta[0] == 1)
    def _():
        for j in range(SEQ_GROUP):
            kt_ref[:, j * TOK : (j + 1) * TOK] = other_ref[j]

    copies = []
    for i in range(PAIRS):
        grad = jnp.dot(
            kt_ref[...], g_ref[:, pair_lanes(i)], preferred_element_type=jnp.float32
        ).astype(jnp.bfloat16)
        stage_ref[2 * i] = grad[:, :TOK]
        stage_ref[2 * i + 1] = grad[:, TOK:]
        pair = pl.ds(2 * i, 2)
        copies.append(pltpu.make_async_copy(stage_ref.at[pair], out_ref.at[pair], sems.at[i]))
        copies[-1].start()
    for copy in copies:
        copy.wait()


def own_key_kernel(meta, sq_ref, g_ref, out_ref):
    grad = key_grad_half(sq_ref, meta[0], g_ref[...])
    for j, lanes in enumerate(BLOCKS):
        out_ref[j] = grad[:, lanes]


def call(kernel, out_specs, out_shape, scratch, mib, flops, args):
    in_vmem = pl.BlockSpec(memory_space=pltpu.VMEM)
    return pl.pallas_call(
        kernel,
        in_specs=[pl.BlockSpec(memory_space=pltpu.SMEM)] + [in_vmem] * (len(args) - 1),
        out_specs=out_specs,
        out_shape=out_shape,
        scratch_shapes=scratch,
        compiler_params=pltpu.CompilerParams(vmem_limit_bytes=mib << 20),
        cost_estimate=pl.CostEstimate(flops=flops, bytes_accessed=8 << 20, transcendentals=1 << 20),
    )(*args)


def on_device(student_query, teacher_query, student_keys, teacher_keys, loss_weight, doc_lengths):
    core = lax.axis_index("c")
    x = lax.axis_index("x")
    me = lax.axis_index(("zi", "y"))
    seq = lax.axis_index(("zo", "zi", "y"))
    meta = jnp.concatenate([jnp.stack([core, me, seq]).astype(jnp.int32), doc_lengths])
    sq = student_query.transpose(1, 2, 0)
    tq = teacher_query.transpose(1, 2, 0)
    lw = loss_weight.T

    table = jnp.where(core == 0, student_keys.T, teacher_keys.T)
    own = lax.dynamic_slice_in_dim(table, x * PIECE, PIECE, 0)
    before = lax.ppermute(own, ("zo", "zi"), [(i, i + 2) for i in range(14)])
    later = (jnp.arange(SEQ_GROUP) >= me)[:, None, None, None]
    outgoing = jnp.broadcast_to(jnp.where(later, own, before), (SEQ_GROUP, 4, PIECE, TOK))
    mine = lax.all_to_all(
        outgoing.reshape(SEQ_GROUP * 4, PIECE, TOK), ("zi", "y", "x"), 0, 0, tiled=True
    ).reshape(SEQ_GROUP, KDIM, TOK)
    other = lax.ppermute(mine, "c", [(0, 1), (1, 0)])

    in_vmem = pl.BlockSpec(memory_space=pltpu.VMEM)
    scratch = [
        pltpu.VMEM((WIN, KDIM), jnp.bfloat16),
        pltpu.VMEM((WIN, TOK), jnp.float32),
        pltpu.VMEM((2, WIN, 2 * TOK), jnp.float32),
    ]
    matmul = 2 * WIN * HEADS * TOK * KDIM
    probs = call(
        first_kernel,
        in_vmem,
        jax.ShapeDtypeStruct((WIN, HEADS * TOK), jnp.float32),
        scratch,
        12,
        matmul,
        (meta, mine, sq, tq, lw),
    )
    half_grad = jax.ShapeDtypeStruct((SEQ_GROUP, HALF, TOK), jnp.bfloat16)
    score_grad, sent = call(
        second_kernel,
        [in_vmem, in_vmem],
        [jax.ShapeDtypeStruct((WIN, HEADS * TOK), jnp.bfloat16), half_grad],
        scratch,
        12,
        matmul * 3 // 2,
        (meta, other, sq, tq, lw, probs),
    )
    got = lax.ppermute(sent, "c", [(0, 1), (1, 0)])
    own_half = call(
        own_key_kernel,
        in_vmem,
        jax.ShapeDtypeStruct((SEQ_GROUP, HALF, TOK), jnp.float32),
        [],
        6,
        matmul // 2,
        (meta, sq, score_grad),
    )
    partial = (own_half + got.astype(jnp.float32)).astype(jnp.bfloat16)
    rows = HALF // 4
    terms = lax.all_to_all(
        partial.reshape(SEQ_GROUP * 4, rows, TOK), ("zi", "y", "x"), 0, 0, tiled=True
    ).reshape(SEQ_GROUP, 4, rows, TOK)
    terms = jnp.sum(terms.astype(jnp.float32), axis=1)
    here = (jnp.arange(SEQ_GROUP) >= me)[:, None, None]
    kept = jnp.sum(jnp.where(here, terms, 0.0), axis=0)
    returned = jnp.sum(jnp.where(here, 0.0, terms), axis=0)
    returned = lax.ppermute(returned, ("zo", "zi"), [(i + 2, i) for i in range(14)])
    query_grad, kept = call(
        query_kernel,
        [pl.BlockSpec(memory_space=pl.ANY), in_vmem],
        [
            jax.ShapeDtypeStruct((HEADS, KDIM, TOK), jnp.bfloat16),
            jax.ShapeDtypeStruct((rows, TOK), jnp.float32),
        ],
        [
            pltpu.VMEM((KDIM, WIN), jnp.bfloat16),
            pltpu.VMEM((HEADS, KDIM, TOK), jnp.bfloat16),
            pltpu.SemaphoreType.DMA((PAIRS,)),
        ],
        8,
        matmul,
        (meta, mine, other, score_grad, kept),
    )
    share = (kept + returned).astype(jnp.bfloat16)
    key_grad = lax.all_to_all(
        jnp.broadcast_to(share, (8, rows, TOK)), ("c", "x"), 0, 0, tiled=True
    ).reshape(KDIM, TOK)
    return (query_grad.transpose(2, 0, 1), key_grad.T)


def solution(mesh):
    fine = Mesh(mesh.devices.reshape(8, 2, 4, 4, 2), ("zo", "zi", "y", "x", "c"))
    seq, head = ("zo", "zi", "y"), ("x", "c")
    return jax.shard_map(
        on_device,
        mesh=fine,
        in_specs=(
            P(seq, head, None),
            P(seq, head, None),
            P(seq, None),
            P(seq, None),
            P(seq, head),
            P(),
        ),
        out_specs=(P(seq, head, None), P(seq, None)),
        check_vma=False,
    )
```

```python
import functools
import math

import jax
import jax.numpy as jnp
from jax import lax
from jax.experimental import pallas as pl
from jax.experimental.pallas import tpu as pltpu
from jax.sharding import Mesh
from jax.sharding import PartitionSpec as P

SEQ_GROUP = 8
TOK = 128
WIN = SEQ_GROUP * TOK
KDIM = 576
HALF = KDIM // 2
PIECE = KDIM // 4
HEADS = 8
PAIRS = HEADS // 2
BLOCKS = [slice(j * TOK, (j + 1) * TOK) for j in range(SEQ_GROUP)]
SCALE = 192.0 ** (-0.5)
SCALE_LOG2 = SCALE * math.log2(math.e)
HIDDEN = -1e30


def document_start(meta):
    query_pos = meta[2] * TOK + lax.broadcasted_iota(jnp.int32, (1, TOK), 1)
    start = jnp.zeros((1, TOK), jnp.int32)
    end = jnp.int32(0)
    for m in range(16):
        end = end + meta[3 + m]
        start = jnp.where(query_pos >= end, end, start)
    return query_pos, start


def key_block(meta, j, positions, kt_ref, k_ref, bias_ref):
    me, seq = meta[1], meta[2]
    query_pos, start = positions
    block = seq - me + j - jnp.where(j > me, SEQ_GROUP, 0)
    key_pos = block * TOK + lax.broadcasted_iota(jnp.int32, (TOK, TOK), 0)
    seen = (key_pos >= start) & (key_pos <= query_pos)
    bias_ref[BLOCKS[j], :] = jnp.where(seen, 0.0, HIDDEN)
    k_ref[BLOCKS[j], :] = kt_ref[j].T


def both(a, b):
    return jnp.concatenate([a, b], axis=1)


def scores(k_ref, bias_ref, queries, s_ref, prepare=None):
    peak = jnp.full((8, 2 * TOK), HIDDEN, jnp.float32)
    for j, rows in enumerate(BLOCKS):
        if prepare is not None:
            prepare(j)
        bias = bias_ref[rows, :]
        s = jnp.dot(k_ref[rows, :], queries, preferred_element_type=jnp.float32)
        s = s + both(bias, bias)
        s_ref[rows, :] = s
        peak = jnp.maximum(peak, jnp.max(s.reshape(TOK // 8, 8, 2 * TOK), axis=0))
    return jnp.max(peak, axis=0, keepdims=True)


def exponentials(s_ref, peak, put):
    total = jnp.zeros((8, 2 * TOK), jnp.float32)
    for rows in BLOCKS:
        e = jnp.exp2((s_ref[rows, :] - peak) * SCALE_LOG2)
        put(rows, e)
        total = total + jnp.sum(e.reshape(TOK // 8, 8, 2 * TOK), axis=0)
    return jnp.sum(total, axis=0, keepdims=True)


def pair_queries(student, sq_ref, tq_ref, i):
    return both(
        jnp.where(student, sq_ref[2 * i], tq_ref[2 * i]),
        jnp.where(student, sq_ref[2 * i + 1], tq_ref[2 * i + 1]),
    )


def pair_weight(lw_ref, i, student):
    weight = both(lw_ref[2 * i : 2 * i + 1, :], lw_ref[2 * i + 1 : 2 * i + 2, :])
    return weight * jnp.where(student, SCALE, -SCALE)


def all_pairs(meta, student, kt_ref, sq_ref, tq_ref, lw_ref, k_ref, bias_ref, s_ref, put, use):
    positions = document_start(meta)
    peak = scores(
        k_ref,
        bias_ref,
        pair_queries(student, sq_ref, tq_ref, 0),
        s_ref.at[0],
        lambda j: key_block(meta, j, positions, kt_ref, k_ref, bias_ref),
    )
    for i in range(PAIRS):
        later = None
        if i + 1 < PAIRS:
            queries = pair_queries(student, sq_ref, tq_ref, i + 1)
            later = scores(k_ref, bias_ref, queries, s_ref.at[(i + 1) % 2])
        total = exponentials(s_ref.at[i % 2], peak, functools.partial(put, i))
        use(i, pair_weight(lw_ref, i, student) / total)
        peak = later


def pair_lanes(i):
    return slice(i * 2 * TOK, (i + 1) * 2 * TOK)


def first_kernel(meta, kt_ref, sq_ref, tq_ref, lw_ref, e_ref, k_ref, bias_ref, s_ref):
    def put(i, rows, e):
        e_ref[rows, pair_lanes(i)] = e

    def use(i, factor):
        e_ref[WIN : WIN + 1, pair_lanes(i)] = factor

    student = meta[0] == 0
    all_pairs(meta, student, kt_ref, sq_ref, tq_ref, lw_ref, k_ref, bias_ref, s_ref, put, use)


def key_grad_half(sq_ref, half, g):
    rows = pl.ds(pl.multiple_of(half * HALF, HALF), HALF)
    queries = jnp.concatenate([sq_ref[h, rows, :] for h in range(HEADS)], axis=1)
    return lax.dot_general(
        queries, g, (((1,), (1,)), ((), ())), preferred_element_type=jnp.float32
    )


def second_kernel(
    meta, kt_ref, sq_ref, tq_ref, lw_ref, e_ref, g_ref, kg_ref, k_ref, bias_ref, s_ref
):
    student = meta[0] == 1

    def put(i, rows, e):
        s_ref[i % 2, rows, :] = e

    def use(i, factor):
        lanes = pair_lanes(i)
        first = e_ref[WIN : WIN + 1, lanes]
        for rows in BLOCKS:
            g = e_ref[rows, lanes] * first + s_ref[i % 2, rows, :] * factor
            g_ref[rows, lanes] = g.astype(jnp.bfloat16)

    all_pairs(meta, student, kt_ref, sq_ref, tq_ref, lw_ref, k_ref, bias_ref, s_ref, put, use)
    grad = key_grad_half(sq_ref, 1 - meta[0], g_ref[...]).astype(jnp.bfloat16)
    for j in range(SEQ_GROUP):
        kg_ref[j] = grad[:, j * TOK : (j + 1) * TOK]


def query_kernel(
    meta, mine_ref, other_ref, g_ref, kept_ref, out_ref, kept_out_ref, kt_ref, stage_ref, sems
):
    kept_out_ref[...] = kept_ref[...]

    @pl.when(meta[0] == 0)
    def _():
        for j in range(SEQ_GROUP):
            kt_ref[:, j * TOK : (j + 1) * TOK] = mine_ref[j]

    @pl.when(meta[0] == 1)
    def _():
        for j in range(SEQ_GROUP):
            kt_ref[:, j * TOK : (j + 1) * TOK] = other_ref[j]

    copies = []
    for i in range(PAIRS):
        grad = jnp.dot(
            kt_ref[...], g_ref[:, pair_lanes(i)], preferred_element_type=jnp.float32
        ).astype(jnp.bfloat16)
        stage_ref[2 * i] = grad[:, :TOK]
        stage_ref[2 * i + 1] = grad[:, TOK:]
        pair = pl.ds(2 * i, 2)
        copies.append(pltpu.make_async_copy(stage_ref.at[pair], out_ref.at[pair], sems.at[i]))
        copies[-1].start()
    for copy in copies:
        copy.wait()


def own_key_kernel(meta, sq_ref, g_ref, out_ref):
    grad = key_grad_half(sq_ref, meta[0], g_ref[...])
    for j, lanes in enumerate(BLOCKS):
        out_ref[j] = grad[:, lanes]


def call(kernel, out_specs, out_shape, scratch, mib, flops, args):
    in_vmem = pl.BlockSpec(memory_space=pltpu.VMEM)
    return pl.pallas_call(
        kernel,
        in_specs=[pl.BlockSpec(memory_space=pltpu.SMEM)] + [in_vmem] * (len(args) - 1),
        out_specs=out_specs,
        out_shape=out_shape,
        scratch_shapes=scratch,
        compiler_params=pltpu.CompilerParams(vmem_limit_bytes=mib << 20),
        cost_estimate=pl.CostEstimate(flops=flops, bytes_accessed=8 << 20, transcendentals=1 << 20),
    )(*args)


def on_device(student_query, teacher_query, student_keys, teacher_keys, loss_weight, doc_lengths):
    core = lax.axis_index("c")
    x = lax.axis_index("x")
    me = lax.axis_index(("zi", "y"))
    seq = lax.axis_index(("zo", "zi", "y"))
    meta = jnp.concatenate([jnp.stack([core, me, seq]).astype(jnp.int32), doc_lengths])
    sq = student_query.transpose(1, 2, 0)
    tq = teacher_query.transpose(1, 2, 0)
    lw = loss_weight.T

    table = jnp.where(core == 0, student_keys.T, teacher_keys.T)
    own = lax.dynamic_slice_in_dim(table, x * PIECE, PIECE, 0)
    before = lax.ppermute(own, ("zo", "zi"), [(i, i + 2) for i in range(14)])
    later = (jnp.arange(SEQ_GROUP) >= me)[:, None, None, None]
    outgoing = jnp.broadcast_to(jnp.where(later, own, before), (SEQ_GROUP, 4, PIECE, TOK))
    mine = lax.all_to_all(
        outgoing.reshape(SEQ_GROUP * 4, PIECE, TOK), ("zi", "y", "x"), 0, 0, tiled=True
    ).reshape(SEQ_GROUP, KDIM, TOK)
    other = lax.ppermute(mine, "c", [(0, 1), (1, 0)])

    in_vmem = pl.BlockSpec(memory_space=pltpu.VMEM)
    scratch = [
        pltpu.VMEM((WIN, KDIM), jnp.bfloat16),
        pltpu.VMEM((WIN, TOK), jnp.float32),
        pltpu.VMEM((2, WIN, 2 * TOK), jnp.float32),
    ]
    matmul = 2 * WIN * HEADS * TOK * KDIM
    first = call(
        first_kernel,
        in_vmem,
        jax.ShapeDtypeStruct((WIN + 8, HEADS * TOK), jnp.float32),
        scratch,
        12,
        matmul,
        (meta, mine, sq, tq, lw),
    )
    half_grad = jax.ShapeDtypeStruct((SEQ_GROUP, HALF, TOK), jnp.bfloat16)
    score_grad, sent = call(
        second_kernel,
        [in_vmem, in_vmem],
        [jax.ShapeDtypeStruct((WIN, HEADS * TOK), jnp.bfloat16), half_grad],
        scratch,
        12,
        matmul * 3 // 2,
        (meta, other, sq, tq, lw, first),
    )
    got = lax.ppermute(sent, "c", [(0, 1), (1, 0)])
    own_half = call(
        own_key_kernel,
        in_vmem,
        jax.ShapeDtypeStruct((SEQ_GROUP, HALF, TOK), jnp.float32),
        [],
        6,
        matmul // 2,
        (meta, sq, score_grad),
    )
    partial = (own_half + got.astype(jnp.float32)).astype(jnp.bfloat16)
    rows = HALF // 4
    terms = lax.all_to_all(
        partial.reshape(SEQ_GROUP * 4, rows, TOK), ("zi", "y", "x"), 0, 0, tiled=True
    ).reshape(SEQ_GROUP, 4, rows, TOK)
    terms = jnp.sum(terms.astype(jnp.float32), axis=1)
    here = (jnp.arange(SEQ_GROUP) >= me)[:, None, None]
    kept = jnp.sum(jnp.where(here, terms, 0.0), axis=0)
    returned = jnp.sum(jnp.where(here, 0.0, terms), axis=0)
    returned = lax.ppermute(returned, ("zo", "zi"), [(i + 2, i) for i in range(14)])
    query_grad, kept = call(
        query_kernel,
        [pl.BlockSpec(memory_space=pl.ANY), in_vmem],
        [
            jax.ShapeDtypeStruct((HEADS, KDIM, TOK), jnp.bfloat16),
            jax.ShapeDtypeStruct((rows, TOK), jnp.float32),
        ],
        [
            pltpu.VMEM((KDIM, WIN), jnp.bfloat16),
            pltpu.VMEM((HEADS, KDIM, TOK), jnp.bfloat16),
            pltpu.SemaphoreType.DMA((PAIRS,)),
        ],
        8,
        matmul,
        (meta, mine, other, score_grad, kept),
    )
    share = (kept + returned).astype(jnp.bfloat16)
    key_grad = lax.all_to_all(
        jnp.broadcast_to(share, (8, rows, TOK)), ("c", "x"), 0, 0, tiled=True
    ).reshape(KDIM, TOK)
    return (query_grad.transpose(2, 0, 1), key_grad.T)


def solution(mesh):
    fine = Mesh(mesh.devices.reshape(8, 2, 4, 4, 2), ("zo", "zi", "y", "x", "c"))
    seq, head = ("zo", "zi", "y"), ("x", "c")
    return jax.shard_map(
        on_device,
        mesh=fine,
        in_specs=(
            P(seq, head, None),
            P(seq, head, None),
            P(seq, None),
            P(seq, None),
            P(seq, head),
            P(),
        ),
        out_specs=(P(seq, head, None), P(seq, None)),
        check_vma=False,
    )
```

```python
import functools
import math

import jax
import jax.numpy as jnp
from jax import lax
from jax.experimental import pallas as pl
from jax.experimental.pallas import tpu as pltpu
from jax.sharding import Mesh
from jax.sharding import PartitionSpec as P

SEQ_GROUP = 8
TOK = 128
WIN = SEQ_GROUP * TOK
KDIM = 576
HALF = KDIM // 2
PIECE = KDIM // 4
HEADS = 8
PAIRS = HEADS // 2
BLOCKS = [slice(j * TOK, (j + 1) * TOK) for j in range(SEQ_GROUP)]
SCALE = 192.0 ** (-0.5)
SCALE_LOG2 = SCALE * math.log2(math.e)
HIDDEN = -1e30


def document_start(meta):
    query_pos = meta[2] * TOK + lax.broadcasted_iota(jnp.int32, (1, TOK), 1)
    start = jnp.zeros((1, TOK), jnp.int32)
    end = jnp.int32(0)
    for m in range(16):
        end = end + meta[3 + m]
        start = jnp.where(query_pos >= end, end, start)
    return query_pos, start


def key_block(meta, j, positions, kt_ref, k_ref, bias_ref):
    me, seq = meta[1], meta[2]
    query_pos, start = positions
    block = seq - me + j - jnp.where(j > me, SEQ_GROUP, 0)
    key_pos = block * TOK + lax.broadcasted_iota(jnp.int32, (TOK, TOK), 0)
    seen = (key_pos >= start) & (key_pos <= query_pos)
    bias_ref[BLOCKS[j], :] = jnp.where(seen, 0.0, HIDDEN)
    k_ref[BLOCKS[j], :] = kt_ref[j].T


def both(a, b):
    return jnp.concatenate([a, b], axis=1)


def scores(k_ref, bias_ref, queries, s_ref, prepare=None):
    peak = jnp.full((8, 2 * TOK), HIDDEN, jnp.float32)
    for j, rows in enumerate(BLOCKS):
        if prepare is not None:
            prepare(j)
        bias = bias_ref[rows, :]
        s = jnp.dot(k_ref[rows, :], queries, preferred_element_type=jnp.float32)
        s = s + both(bias, bias)
        s_ref[rows, :] = s
        peak = jnp.maximum(peak, jnp.max(s.reshape(TOK // 8, 8, 2 * TOK), axis=0))
    return jnp.max(peak, axis=0, keepdims=True)


def exponentials(s_ref, peak, put):
    total = jnp.zeros((8, 2 * TOK), jnp.float32)
    for rows in BLOCKS:
        e = jnp.exp2((s_ref[rows, :] - peak) * SCALE_LOG2)
        put(rows, e)
        total = total + jnp.sum(e.reshape(TOK // 8, 8, 2 * TOK), axis=0)
    return jnp.sum(total, axis=0, keepdims=True)


def pair_queries(student, sq_ref, tq_ref, i):
    return both(
        jnp.where(student, sq_ref[2 * i], tq_ref[2 * i]),
        jnp.where(student, sq_ref[2 * i + 1], tq_ref[2 * i + 1]),
    )


def pair_weight(lw_ref, i, student):
    weight = both(lw_ref[2 * i : 2 * i + 1, :], lw_ref[2 * i + 1 : 2 * i + 2, :])
    return weight * jnp.where(student, SCALE, -SCALE)


def all_pairs(meta, student, kt_ref, sq_ref, tq_ref, lw_ref, k_ref, bias_ref, s_ref, put, use):
    positions = document_start(meta)
    peak = scores(
        k_ref,
        bias_ref,
        pair_queries(student, sq_ref, tq_ref, 0),
        s_ref.at[0],
        lambda j: key_block(meta, j, positions, kt_ref, k_ref, bias_ref),
    )
    for i in range(PAIRS):
        later = None
        if i + 1 < PAIRS:
            queries = pair_queries(student, sq_ref, tq_ref, i + 1)
            later = scores(k_ref, bias_ref, queries, s_ref.at[(i + 1) % 2])
        total = exponentials(s_ref.at[i % 2], peak, functools.partial(put, i))
        use(i, pair_weight(lw_ref, i, student) / total)
        peak = later


def pair_lanes(i):
    return slice(i * 2 * TOK, (i + 1) * 2 * TOK)


def first_kernel(meta, kt_ref, sq_ref, tq_ref, lw_ref, e_ref, k_ref, bias_ref, s_ref):
    def put(i, rows, e):
        e_ref[rows, pair_lanes(i)] = e

    def use(i, factor):
        e_ref[WIN : WIN + 1, pair_lanes(i)] = factor

    student = meta[0] == 0
    all_pairs(meta, student, kt_ref, sq_ref, tq_ref, lw_ref, k_ref, bias_ref, s_ref, put, use)


def key_grad_half(sq_ref, half, g):
    rows = pl.ds(pl.multiple_of(half * HALF, HALF), HALF)
    queries = jnp.concatenate([sq_ref[h, rows, :] for h in range(HEADS)], axis=1)
    return lax.dot_general(
        queries, g, (((1,), (1,)), ((), ())), preferred_element_type=jnp.float32
    )


def second_kernel(
    meta, kt_ref, sq_ref, tq_ref, lw_ref, e_ref, g_ref, kg_ref, k_ref, bias_ref, s_ref
):
    student = meta[0] == 1

    def put(i, rows, e):
        s_ref[i % 2, rows, :] = e

    def use(i, factor):
        lanes = pair_lanes(i)
        first = e_ref[WIN : WIN + 1, lanes]
        for rows in BLOCKS:
            g = e_ref[rows, lanes] * first + s_ref[i % 2, rows, :] * factor
            g_ref[rows, lanes] = g.astype(jnp.bfloat16)

    all_pairs(meta, student, kt_ref, sq_ref, tq_ref, lw_ref, k_ref, bias_ref, s_ref, put, use)
    grad = key_grad_half(sq_ref, 1 - meta[0], g_ref[...]).astype(jnp.bfloat16)
    for j in range(SEQ_GROUP):
        kg_ref[j] = grad[:, j * TOK : (j + 1) * TOK]


def query_kernel(
    meta, mine_ref, other_ref, g_ref, kept_ref, out_ref, kept_out_ref, kt_ref, stage_ref, sems
):
    kept_out_ref[...] = kept_ref[...]

    @pl.when(meta[0] == 0)
    def _():
        for j in range(SEQ_GROUP):
            kt_ref[:, j * TOK : (j + 1) * TOK] = mine_ref[j]

    @pl.when(meta[0] == 1)
    def _():
        for j in range(SEQ_GROUP):
            kt_ref[:, j * TOK : (j + 1) * TOK] = other_ref[j]

    copies = []
    for i in range(PAIRS):
        grad = jnp.dot(
            kt_ref[...], g_ref[:, pair_lanes(i)], preferred_element_type=jnp.float32
        ).astype(jnp.bfloat16)
        stage_ref[2 * i] = grad[:, :TOK]
        stage_ref[2 * i + 1] = grad[:, TOK:]
        pair = pl.ds(2 * i, 2)
        copies.append(pltpu.make_async_copy(stage_ref.at[pair], out_ref.at[pair], sems.at[i]))
        copies[-1].start()
    for copy in copies:
        copy.wait()


def own_key_kernel(meta, sq_ref, g_ref, out_ref):
    grad = key_grad_half(sq_ref, meta[0], g_ref[...])
    for j, lanes in enumerate(BLOCKS):
        out_ref[j] = grad[:, lanes]


def call(kernel, out_specs, out_shape, scratch, mib, flops, args):
    in_vmem = pl.BlockSpec(memory_space=pltpu.VMEM)
    return pl.pallas_call(
        kernel,
        in_specs=[pl.BlockSpec(memory_space=pltpu.SMEM)] + [in_vmem] * (len(args) - 1),
        out_specs=out_specs,
        out_shape=out_shape,
        scratch_shapes=scratch,
        compiler_params=pltpu.CompilerParams(vmem_limit_bytes=mib << 20),
        cost_estimate=pl.CostEstimate(flops=flops, bytes_accessed=8 << 20, transcendentals=1 << 20),
    )(*args)


def on_device(student_query, teacher_query, student_keys, teacher_keys, loss_weight, doc_lengths):
    core = lax.axis_index("c")
    x = lax.axis_index("x")
    me = lax.axis_index(("zi", "y"))
    seq = lax.axis_index(("zo", "zi", "y"))
    meta = jnp.concatenate([jnp.stack([core, me, seq]).astype(jnp.int32), doc_lengths])
    sq = student_query.transpose(1, 2, 0)
    tq = teacher_query.transpose(1, 2, 0)
    lw = loss_weight.T

    table = jnp.where(core == 0, student_keys.T, teacher_keys.T)
    own = lax.dynamic_slice_in_dim(table, x * PIECE, PIECE, 0)
    before = lax.ppermute(own, ("zo", "zi"), [(i, i + 2) for i in range(14)])
    later = (jnp.arange(SEQ_GROUP) >= me)[:, None, None, None]
    outgoing = jnp.broadcast_to(jnp.where(later, own, before), (SEQ_GROUP, 4, PIECE, TOK))
    mine = lax.all_to_all(
        outgoing.reshape(SEQ_GROUP * 4, PIECE, TOK), ("zi", "y", "x"), 0, 0, tiled=True
    ).reshape(SEQ_GROUP, KDIM, TOK)
    other = lax.ppermute(mine, "c", [(0, 1), (1, 0)])

    in_vmem = pl.BlockSpec(memory_space=pltpu.VMEM)
    scratch = [
        pltpu.VMEM((WIN, KDIM), jnp.bfloat16),
        pltpu.VMEM((WIN, TOK), jnp.float32),
        pltpu.VMEM((2, WIN, 2 * TOK), jnp.float32),
    ]
    matmul = 2 * WIN * HEADS * TOK * KDIM
    first = call(
        first_kernel,
        in_vmem,
        jax.ShapeDtypeStruct((WIN + 8, HEADS * TOK), jnp.float32),
        scratch,
        12,
        matmul,
        (meta, mine, sq, tq, lw),
    )
    half_grad = jax.ShapeDtypeStruct((SEQ_GROUP, HALF, TOK), jnp.bfloat16)
    score_grad, sent = call(
        second_kernel,
        [in_vmem, in_vmem],
        [jax.ShapeDtypeStruct((WIN, HEADS * TOK), jnp.bfloat16), half_grad],
        scratch,
        12,
        matmul * 3 // 2,
        (meta, other, sq, tq, lw, first),
    )
    got = lax.ppermute(sent, "c", [(0, 1), (1, 0)])
    own_half = call(
        own_key_kernel,
        in_vmem,
        jax.ShapeDtypeStruct((SEQ_GROUP, HALF, TOK), jnp.float32),
        [],
        6,
        matmul // 2,
        (meta, sq, score_grad),
    )
    partial = (own_half + got.astype(jnp.float32)).astype(jnp.bfloat16)
    rows = HALF // 4
    terms = lax.all_to_all(
        partial.reshape(SEQ_GROUP * 4, rows, TOK), ("zi", "y", "x"), 0, 0, tiled=True
    ).reshape(SEQ_GROUP, 4, rows, TOK)
    terms = jnp.sum(terms.astype(jnp.float32), axis=1)
    here = (jnp.arange(SEQ_GROUP) >= me)[:, None, None]
    kept = jnp.sum(jnp.where(here, terms, 0.0), axis=0)
    returned = jnp.sum(jnp.where(here, 0.0, terms), axis=0)
    returned = lax.ppermute(returned.astype(jnp.bfloat16), ("zo", "zi"), [(i + 2, i) for i in range(14)])
    query_grad, kept = call(
        query_kernel,
        [pl.BlockSpec(memory_space=pl.ANY), in_vmem],
        [
            jax.ShapeDtypeStruct((HEADS, KDIM, TOK), jnp.bfloat16),
            jax.ShapeDtypeStruct((rows, TOK), jnp.float32),
        ],
        [
            pltpu.VMEM((KDIM, WIN), jnp.bfloat16),
            pltpu.VMEM((HEADS, KDIM, TOK), jnp.bfloat16),
            pltpu.SemaphoreType.DMA((PAIRS,)),
        ],
        8,
        matmul,
        (meta, mine, other, score_grad, kept),
    )
    share = (kept + returned.astype(jnp.float32)).astype(jnp.bfloat16)
    key_grad = lax.all_to_all(
        jnp.broadcast_to(share, (8, rows, TOK)), ("c", "x"), 0, 0, tiled=True
    ).reshape(KDIM, TOK)
    return (query_grad.transpose(2, 0, 1), key_grad.T)


def solution(mesh):
    fine = Mesh(mesh.devices.reshape(8, 2, 4, 4, 2), ("zo", "zi", "y", "x", "c"))
    seq, head = ("zo", "zi", "y"), ("x", "c")
    return jax.shard_map(
        on_device,
        mesh=fine,
        in_specs=(
            P(seq, head, None),
            P(seq, head, None),
            P(seq, None),
            P(seq, None),
            P(seq, head),
            P(),
        ),
        out_specs=(P(seq, head, None), P(seq, None)),
        check_vma=False,
    )
```

```python
import functools
import math

import jax
import jax.numpy as jnp
from jax import lax
from jax.experimental import pallas as pl
from jax.experimental.pallas import tpu as pltpu
from jax.sharding import Mesh
from jax.sharding import PartitionSpec as P

SEQ_GROUP = 8
TOK = 128
WIN = SEQ_GROUP * TOK
KDIM = 576
HALF = KDIM // 2
PIECE = KDIM // 4
HEADS = 8
PAIRS = HEADS // 2
BLOCKS = [slice(j * TOK, (j + 1) * TOK) for j in range(SEQ_GROUP)]
SCALE = 192.0 ** (-0.5)
SCALE_LOG2 = SCALE * math.log2(math.e)
HIDDEN = -1e30


def document_start(meta):
    query_pos = meta[2] * TOK + lax.broadcasted_iota(jnp.int32, (1, TOK), 1)
    start = jnp.zeros((1, TOK), jnp.int32)
    end = jnp.int32(0)
    for m in range(16):
        end = end + meta[3 + m]
        start = jnp.where(query_pos >= end, end, start)
    return query_pos, start


def key_block(meta, j, positions, kt_ref, k_ref, bias_ref):
    me, seq = meta[1], meta[2]
    query_pos, start = positions
    block = seq - me + j - jnp.where(j > me, SEQ_GROUP, 0)
    key_pos = block * TOK + lax.broadcasted_iota(jnp.int32, (TOK, TOK), 0)
    seen = (key_pos >= start) & (key_pos <= query_pos)
    bias_ref[BLOCKS[j], :] = jnp.where(seen, 0.0, HIDDEN)
    k_ref[BLOCKS[j], :] = kt_ref[j].T


def both(a, b):
    return jnp.concatenate([a, b], axis=1)


def scores(k_ref, bias_ref, queries, s_ref, prepare=None):
    peak = jnp.full((8, 2 * TOK), HIDDEN, jnp.float32)
    for j, rows in enumerate(BLOCKS):
        if prepare is not None:
            prepare(j)
        bias = bias_ref[rows, :]
        s = jnp.dot(k_ref[rows, :], queries, preferred_element_type=jnp.float32)
        s = s + both(bias, bias)
        s_ref[rows, :] = s
        peak = jnp.maximum(peak, jnp.max(s.reshape(TOK // 8, 8, 2 * TOK), axis=0))
    return jnp.max(peak, axis=0, keepdims=True)


def exponentials(s_ref, peak, put):
    total = jnp.zeros((8, 2 * TOK), jnp.float32)
    for rows in BLOCKS:
        e = jnp.exp2((s_ref[rows, :] - peak) * SCALE_LOG2)
        put(rows, e)
        total = total + jnp.sum(e.reshape(TOK // 8, 8, 2 * TOK), axis=0)
    return jnp.sum(total, axis=0, keepdims=True)


def pair_queries(student, sq_ref, tq_ref, i):
    return both(
        jnp.where(student, sq_ref[2 * i], tq_ref[2 * i]),
        jnp.where(student, sq_ref[2 * i + 1], tq_ref[2 * i + 1]),
    )


def pair_weight(lw_ref, i, student):
    weight = both(lw_ref[2 * i : 2 * i + 1, :], lw_ref[2 * i + 1 : 2 * i + 2, :])
    return weight * jnp.where(student, SCALE, -SCALE)


def all_pairs(meta, student, kt_ref, sq_ref, tq_ref, lw_ref, k_ref, bias_ref, s_ref, put, use):
    positions = document_start(meta)
    peak = scores(
        k_ref,
        bias_ref,
        pair_queries(student, sq_ref, tq_ref, 0),
        s_ref.at[0],
        lambda j: key_block(meta, j, positions, kt_ref, k_ref, bias_ref),
    )
    for i in range(PAIRS):
        later = None
        if i + 1 < PAIRS:
            queries = pair_queries(student, sq_ref, tq_ref, i + 1)
            later = scores(k_ref, bias_ref, queries, s_ref.at[(i + 1) % 2])
        total = exponentials(s_ref.at[i % 2], peak, functools.partial(put, i))
        use(i, pair_weight(lw_ref, i, student) / total)
        peak = later


def pair_lanes(i):
    return slice(i * 2 * TOK, (i + 1) * 2 * TOK)


def first_kernel(meta, kt_ref, sq_ref, tq_ref, lw_ref, e_ref, k_ref, bias_ref, s_ref):
    def put(i, rows, e):
        e_ref[rows, pair_lanes(i)] = e

    def use(i, factor):
        e_ref[WIN : WIN + 1, pair_lanes(i)] = factor

    student = meta[0] == 0
    all_pairs(meta, student, kt_ref, sq_ref, tq_ref, lw_ref, k_ref, bias_ref, s_ref, put, use)


def key_grad_half(sq_ref, half, g):
    rows = pl.ds(pl.multiple_of(half * HALF, HALF), HALF)
    queries = jnp.concatenate([sq_ref[h, rows, :] for h in range(HEADS)], axis=1)
    return lax.dot_general(
        queries, g, (((1,), (1,)), ((), ())), preferred_element_type=jnp.float32
    )


def second_kernel(
    meta, kt_ref, sq_ref, tq_ref, lw_ref, e_ref, g_ref, kg_ref, k_ref, bias_ref, s_ref
):
    student = meta[0] == 1

    def put(i, rows, e):
        s_ref[i % 2, rows, :] = e

    def use(i, factor):
        lanes = pair_lanes(i)
        first = e_ref[WIN : WIN + 1, lanes]
        for rows in BLOCKS:
            g = e_ref[rows, lanes] * first + s_ref[i % 2, rows, :] * factor
            g_ref[rows, lanes] = g.astype(jnp.bfloat16)

    all_pairs(meta, student, kt_ref, sq_ref, tq_ref, lw_ref, k_ref, bias_ref, s_ref, put, use)
    grad = key_grad_half(sq_ref, 1 - meta[0], g_ref[...]).astype(jnp.bfloat16)
    for j in range(SEQ_GROUP):
        kg_ref[j] = grad[:, j * TOK : (j + 1) * TOK]


def query_kernel(
    meta, mine_ref, other_ref, g_ref, kept_ref, out_ref, kept_out_ref, kt_ref, stage_ref, sems, key_sems
):
    kept_out_ref[...] = kept_ref[...]

    def fetch(keys_ref):
        fetched = [
            pltpu.make_async_copy(keys_ref.at[j], kt_ref.at[:, lanes], key_sems.at[j])
            for j, lanes in enumerate(BLOCKS)
        ]
        for copy in fetched:
            copy.start()
        for copy in fetched:
            copy.wait()

    pl.when(meta[0] == 0)(lambda: fetch(mine_ref))
    pl.when(meta[0] == 1)(lambda: fetch(other_ref))

    copies = []
    for i in range(PAIRS):
        grad = jnp.dot(
            kt_ref[...], g_ref[:, pair_lanes(i)], preferred_element_type=jnp.float32
        ).astype(jnp.bfloat16)
        stage_ref[2 * i] = grad[:, :TOK]
        stage_ref[2 * i + 1] = grad[:, TOK:]
        pair = pl.ds(2 * i, 2)
        copies.append(pltpu.make_async_copy(stage_ref.at[pair], out_ref.at[pair], sems.at[i]))
        copies[-1].start()
    for copy in copies:
        copy.wait()


def own_key_kernel(meta, sq_ref, g_ref, out_ref):
    grad = key_grad_half(sq_ref, meta[0], g_ref[...])
    for j, lanes in enumerate(BLOCKS):
        out_ref[j] = grad[:, lanes]


def call(kernel, out_specs, out_shape, scratch, mib, flops, args, left=0):
    in_vmem = pl.BlockSpec(memory_space=pltpu.VMEM)
    return pl.pallas_call(
        kernel,
        in_specs=[pl.BlockSpec(memory_space=pltpu.SMEM)]
        + [pl.BlockSpec(memory_space=pl.ANY)] * left
        + [in_vmem] * (len(args) - 1 - left),
        out_specs=out_specs,
        out_shape=out_shape,
        scratch_shapes=scratch,
        compiler_params=pltpu.CompilerParams(vmem_limit_bytes=mib << 20),
        cost_estimate=pl.CostEstimate(flops=flops, bytes_accessed=8 << 20, transcendentals=1 << 20),
    )(*args)


def on_device(student_query, teacher_query, student_keys, teacher_keys, loss_weight, doc_lengths):
    core = lax.axis_index("c")
    x = lax.axis_index("x")
    me = lax.axis_index(("zi", "y"))
    seq = lax.axis_index(("zo", "zi", "y"))
    meta = jnp.concatenate([jnp.stack([core, me, seq]).astype(jnp.int32), doc_lengths])
    sq = student_query.transpose(1, 2, 0)
    tq = teacher_query.transpose(1, 2, 0)
    lw = loss_weight.T

    table = jnp.where(core == 0, student_keys.T, teacher_keys.T)
    own = lax.dynamic_slice_in_dim(table, x * PIECE, PIECE, 0)
    before = lax.ppermute(own, ("zo", "zi"), [(i, i + 2) for i in range(14)])
    later = (jnp.arange(SEQ_GROUP) >= me)[:, None, None, None]
    outgoing = jnp.broadcast_to(jnp.where(later, own, before), (SEQ_GROUP, 4, PIECE, TOK))
    mine = lax.all_to_all(
        outgoing.reshape(SEQ_GROUP * 4, PIECE, TOK), ("zi", "y", "x"), 0, 0, tiled=True
    ).reshape(SEQ_GROUP, KDIM, TOK)
    other = lax.ppermute(mine, "c", [(0, 1), (1, 0)])

    in_vmem = pl.BlockSpec(memory_space=pltpu.VMEM)
    scratch = [
        pltpu.VMEM((WIN, KDIM), jnp.bfloat16),
        pltpu.VMEM((WIN, TOK), jnp.float32),
        pltpu.VMEM((2, WIN, 2 * TOK), jnp.float32),
    ]
    matmul = 2 * WIN * HEADS * TOK * KDIM
    first = call(
        first_kernel,
        in_vmem,
        jax.ShapeDtypeStruct((WIN + 8, HEADS * TOK), jnp.float32),
        scratch,
        12,
        matmul,
        (meta, mine, sq, tq, lw),
    )
    half_grad = jax.ShapeDtypeStruct((SEQ_GROUP, HALF, TOK), jnp.bfloat16)
    score_grad, sent = call(
        second_kernel,
        [in_vmem, in_vmem],
        [jax.ShapeDtypeStruct((WIN, HEADS * TOK), jnp.bfloat16), half_grad],
        scratch,
        12,
        matmul * 3 // 2,
        (meta, other, sq, tq, lw, first),
    )
    got = lax.ppermute(sent, "c", [(0, 1), (1, 0)])
    own_half = call(
        own_key_kernel,
        in_vmem,
        jax.ShapeDtypeStruct((SEQ_GROUP, HALF, TOK), jnp.float32),
        [],
        6,
        matmul // 2,
        (meta, sq, score_grad),
    )
    partial = (own_half + got.astype(jnp.float32)).astype(jnp.bfloat16)
    rows = HALF // 4
    terms = lax.all_to_all(
        partial.reshape(SEQ_GROUP * 4, rows, TOK), ("zi", "y", "x"), 0, 0, tiled=True
    ).reshape(SEQ_GROUP, 4, rows, TOK)
    terms = jnp.sum(terms.astype(jnp.float32), axis=1)
    here = (jnp.arange(SEQ_GROUP) >= me)[:, None, None]
    kept = jnp.sum(jnp.where(here, terms, 0.0), axis=0)
    returned = jnp.sum(jnp.where(here, 0.0, terms), axis=0)
    returned = lax.ppermute(returned.astype(jnp.bfloat16), ("zo", "zi"), [(i + 2, i) for i in range(14)])
    query_grad, kept = call(
        query_kernel,
        [pl.BlockSpec(memory_space=pl.ANY), in_vmem],
        [
            jax.ShapeDtypeStruct((HEADS, KDIM, TOK), jnp.bfloat16),
            jax.ShapeDtypeStruct((rows, TOK), jnp.float32),
        ],
        [
            pltpu.VMEM((KDIM, WIN), jnp.bfloat16),
            pltpu.VMEM((HEADS, KDIM, TOK), jnp.bfloat16),
            pltpu.SemaphoreType.DMA((PAIRS,)),
            pltpu.SemaphoreType.DMA((SEQ_GROUP,)),
        ],
        8,
        matmul,
        (meta, mine, other, score_grad, kept),
        left=2,
    )
    share = (kept + returned.astype(jnp.float32)).astype(jnp.bfloat16)
    key_grad = lax.all_to_all(
        jnp.broadcast_to(share, (8, rows, TOK)), ("c", "x"), 0, 0, tiled=True
    ).reshape(KDIM, TOK)
    return (query_grad.transpose(2, 0, 1), key_grad.T)


def solution(mesh):
    fine = Mesh(mesh.devices.reshape(8, 2, 4, 4, 2), ("zo", "zi", "y", "x", "c"))
    seq, head = ("zo", "zi", "y"), ("x", "c")
    return jax.shard_map(
        on_device,
        mesh=fine,
        in_specs=(
            P(seq, head, None),
            P(seq, head, None),
            P(seq, None),
            P(seq, None),
            P(seq, head),
            P(),
        ),
        out_specs=(P(seq, head, None), P(seq, None)),
        check_vma=False,
    )
```
